32 devices in a mesh: section: 4 (over z), tm: 4 (over y, x), batch: 2 (over core).
Axes of the slice: x: 2, y: 2, z: 4, core: 2. Of those that a mesh axis runs over, the one named last changes fastest.
Arguments:
- acts: bfloat16 [4, 4, 8, 6, 10240], P('section', 'batch', 'tm'), may hold values from -6 to 6
- cot: bfloat16 [4, 8, 6, 10240], P('batch', 'tm'), may hold values from -6 to 6
- spatial_weight: bfloat16 [4, 9, 64, 64], P('section'), may hold values from -0.25 to 0.25
- temporal_weight: bfloat16 [4, 3, 64, 64], P('section'), may hold values from -0.4375 to 0.4375
Outputs:
- grad_in: bfloat16 [4, 4, 8, 6, 10240], P('section', 'batch', 'tm')
- grad_spatial: float32 [4, 9, 64, 64], P('section')
- grad_temporal: float32 [4, 3, 64, 64], P('section')
The draws below stay inside these ranges and needn't reach their ends.
All inputs are finite; a program needn't handle non-finite values.
Results may differ from the reference program's by a relative error of at most 0.012.
Values may be sent and summed in bfloat16 or wider, within the bound.
A program may use at most 128 MiB of HBM per device.

```python
import jax
import jax.numpy as jnp

C = 64
W = 160
H = 6
TIME_DILATION = 2
SECTIONS = 4
SAMPLE_BINS = 8
SAMPLES = 4


def block_scale(own_key, extent, pieces, low, largest):
    gain = 1.0
    for dim, blocks in pieces:
        draws = jax.random.uniform(jax.random.fold_in(jax.random.fold_in(own_key, 6), dim), (blocks,), jnp.float32, low / len(pieces), largest / len(pieces))
        gain = gain * jnp.repeat(jnp.exp(draws), extent[dim] // blocks).reshape((-1,) + (1,) * (len(extent) - 1 - dim))
    return gain


def scatter_about(key, extent, deviation, most, split=(), held_as=jnp.bfloat16):
    array = jax.random.normal(key, extent, jnp.float32) * deviation
    if len(split) > 0:
        array = block_scale(key, extent, split, -0.22, 0.18) * array
    return jnp.clip(array, min=-most, max=most).astype(held_as)


def setup_inputs(seed: int = 0) -> dict:
    arg_keys = jax.random.split(jax.random.key(seed), 5)
    return {
        "acts": scatter_about(arg_keys[0], (SECTIONS, SAMPLES, SAMPLE_BINS, H, W * C), 1.0, 6.0, ((0, 4), (1, 2), (2, 4))),
        "cot": scatter_about(arg_keys[1], (SAMPLES, SAMPLE_BINS, H, W * C), 1.0, 6.0, ((0, 2), (1, 4))),
        "spatial_weight": scatter_about(arg_keys[2], (SECTIONS, 9, C, C), (9 * C) ** -0.5, 0.25, ((0, 4),)),
        "temporal_weight": scatter_about(arg_keys[3], (SECTIONS, 3, C, C), (3 * C) ** -0.5, 0.4375, ((0, 4),)),
    }


def split_pixels(a, chans):
    return a.reshape(a.shape[:-1] + (a.shape[-1] // chans, chans))


def spatial_fwd(x, ws):
    rows, width = x.shape[1], x.shape[2]
    chans = ws.shape[-1]
    padded = jnp.pad(x, ((0, 0), (1, 1), (chans, chans))).astype(jnp.float32)
    total = jnp.zeros(x.shape, jnp.float32)
    for i in range(3):
        for j in range(3):
            piece = split_pixels(padded[:, i:i + rows, j * chans:j * chans + width], chans)
            total = total + jnp.einsum("nrwc,cd->nrwd", piece, ws[3 * i + j].astype(jnp.float32)).reshape(x.shape)
    return total


def spatial_back(gz, x, ws):
    rows, width = x.shape[1], x.shape[2]
    chans = ws.shape[-1]
    xpad = jnp.pad(x, ((0, 0), (1, 1), (chans, chans))).astype(jnp.float32)
    gradient_padded = jnp.pad(gz, ((0, 0), (1, 1), (chans, chans))).astype(jnp.float32)
    gz_pix = split_pixels(gz.astype(jnp.float32), chans)
    total = jnp.zeros(x.shape, jnp.float32)
    grads = []
    for i in range(3):
        for j in range(3):
            gpiece = split_pixels(gradient_padded[:, 2 - i:2 - i + rows, (2 - j) * chans:(2 - j) * chans + width], chans)
            total = total + jnp.einsum("nrwd,cd->nrwc", gpiece, ws[3 * i + j].astype(jnp.float32)).reshape(x.shape)
            xpiece = split_pixels(xpad[:, i:i + rows, j * chans:j * chans + width], chans)
            grads.append(jnp.einsum("nrwc,nrwd->cd", xpiece, gz_pix))
    return total, jnp.stack(grads)


def reference(acts, cot, spatial_weight, temporal_weight):
    chans = spatial_weight.shape[-1]
    gradient_piece = cot
    outs_in, outs_sp, outs_tm = [], [], []
    for s in range(SECTIONS - 1, -1, -1):
        x = acts[s].reshape((SAMPLES * SAMPLE_BINS, H, W * C))
        z = spatial_fwd(x, spatial_weight[s])
        sig = jax.nn.sigmoid(z)
        h = (z * sig).astype(jnp.bfloat16).reshape(cot.shape)
        deriv = sig * (1.0 + z * (1.0 - sig))
        gradient_padded = jnp.pad(gradient_piece, ((0, 0), (TIME_DILATION, TIME_DILATION), (0, 0), (0, 0)))
        kernel_taps = [gradient_padded[:, 2 * TIME_DILATION:2 * TIME_DILATION + SAMPLE_BINS], gradient_piece, gradient_padded[:, 0:SAMPLE_BINS]]
        wt = temporal_weight[s].astype(jnp.float32)
        gh = jnp.zeros(cot.shape, jnp.float32)
        h_pix = split_pixels(h.astype(jnp.float32), chans)
        tgrads = []
        for k in range(3):
            tap = split_pixels(kernel_taps[k].astype(jnp.float32), chans)
            gh = gh + jnp.einsum("ntrwd,cd->ntrwc", tap, wt[k]).reshape(cot.shape)
            tgrads.append(jnp.einsum("ntrwc,ntrwd->cd", h_pix, tap))
        gh = gh.astype(jnp.bfloat16).reshape(x.shape)
        gz = (gh.astype(jnp.float32) * deriv).astype(jnp.bfloat16)
        back, sgrads = spatial_back(gz, x, spatial_weight[s])
        gradient_piece = (gradient_piece.astype(jnp.float32).reshape(x.shape) + back).astype(jnp.bfloat16).reshape(cot.shape)
        outs_in.append(gradient_piece)
        outs_sp.append(sgrads)
        outs_tm.append(jnp.stack(tgrads))
    return (jnp.stack(outs_in[::-1]), jnp.stack(outs_sp[::-1]), jnp.stack(outs_tm[::-1]))
```

```python
import functools

import jax
import jax.numpy as jnp
from jax import lax
from jax.experimental import pallas as pl
from jax.experimental.pallas import tpu as pltpu
from jax.sharding import PartitionSpec as P

DILATION = 2
ROWS = 8
LANES = 128
HALO = 3


def neighbours(x):
    none = jnp.zeros_like(x[:, :1])
    after = jnp.concatenate([x[:, 1:], none], axis=1)
    before = jnp.concatenate([none, x[:, :-1]], axis=1)
    lane = lax.broadcasted_iota(jnp.int32, x.shape, 3)
    return jnp.where(lane < LANES // 2, after, before)


def flat(x):
    return x.reshape(-1, x.shape[-1])


def mm(a, b, dims):
    return lax.dot_general(a, b, (dims, ((), ())), preferred_element_type=jnp.float32)


def kernel(tiles, frame_pairs, x_ref, w_ref, out_ref, gs, ds):
    sections, bins = x_ref.shape[:2]
    chans = w_ref.shape[-1]
    pairs = gs.shape[1]
    ext = pairs * ROWS
    share = x_ref.shape[2] - ext
    piece = out_ref.shape[2] - tiles * ROWS - (tiles * ROWS) % 16
    tile_rows = out_ref.shape[2] - piece
    out_pairs = tile_rows // ROWS
    first = lax.axis_index("tm") * tiles - HALO
    shape = (bins, pairs, ROWS, LANES)
    place = first + lax.broadcasted_iota(jnp.int32, shape, 1)
    row = lax.broadcasted_iota(jnp.int32, shape, 2)
    inside = (place >= 0) & (place < frame_pairs) & (row < 6)
    zero = jnp.zeros((chans, chans), jnp.bfloat16)
    blank = jnp.zeros((1, pairs, ROWS, LANES), jnp.float32)
    centre = slice(HALO, HALO + tiles)

    wide = [
        jnp.concatenate([x_ref[s, n, ext:, :] for s in range(sections)], axis=0)
        for n in range(bins)
    ]
    g = jnp.stack([v[:ext].astype(jnp.float32).reshape(pairs, ROWS, LANES) for v in wide])
    for s in range(sections - 1, -1, -1):
        w = [w_ref[s, t] for t in range(12)]
        x = x_ref[s, :, 0:ext, :].astype(jnp.float32).reshape(shape)
        xx = jnp.concatenate([x, neighbours(x)], axis=3).astype(jnp.bfloat16)
        fwd = jnp.concatenate(
            [
                jnp.concatenate(
                    [
                        jnp.concatenate([w[3 * i + 1], w[3 * i]], axis=1),
                        jnp.concatenate([w[3 * i + 2], w[3 * i + 1]], axis=1),
                        jnp.concatenate([zero, w[3 * i + 2]], axis=1),
                        jnp.concatenate([w[3 * i], zero], axis=1),
                    ],
                    axis=0,
                )
                for i in range(3)
            ],
            axis=1,
        )
        back = jnp.concatenate(
            [
                jnp.concatenate(
                    [
                        jnp.concatenate([w[3 * i + 1], w[3 * i], zero, w[3 * i + 2]], axis=1),
                        jnp.concatenate([w[3 * i + 2], w[3 * i + 1], w[3 * i], zero], axis=1),
                    ],
                    axis=0,
                )
                for i in range(3)
            ],
            axis=1,
        )
        time = jnp.concatenate(
            [
                jnp.concatenate([w[9], zero, w[10], zero, w[11], zero], axis=1),
                jnp.concatenate([zero, w[9], zero, w[10], zero, w[11]], axis=1),
            ],
            axis=0,
        )
        y = mm(flat(xx), fwd, ((1,), (0,)))
        part = [y[:, LANES * i : LANES * (i + 1)].reshape(-1, ROWS, LANES) for i in range(3)]
        z = part[1] + pltpu.roll(part[0], 1, 1) + pltpu.roll(part[2], ROWS - 1, 1)
        z = z.reshape(shape)
        sig = jax.nn.sigmoid(z)
        h = (z * sig).astype(jnp.bfloat16)
        slope = sig * (1.0 + z * (1.0 - sig))
        after = jnp.concatenate([g[1:], blank], axis=0)
        before = jnp.concatenate([blank, g[:-1]], axis=0)
        g3 = jnp.concatenate([after, g, before], axis=3).astype(jnp.bfloat16)
        gh = mm(flat(g3), time, ((1,), (1,))).astype(jnp.bfloat16)
        gz = (gh.astype(jnp.float32).reshape(shape) * slope).astype(jnp.bfloat16)
        gz = gz.astype(jnp.float32)
        flat_gz = gz.reshape(-1, ROWS, LANES)
        gg = [
            pltpu.roll(flat_gz, ROWS - 1, 1).reshape(shape),
            gz,
            pltpu.roll(flat_gz, 1, 1).reshape(shape),
        ]
        sides = []
        for v in gg:
            sides += [v, neighbours(v)]
        gsides = jnp.concatenate(sides, axis=3).astype(jnp.bfloat16)
        gs_in = mm(flat(gsides), back, ((1,), (1,))).reshape(shape)
        result = jnp.where(inside, g + gs_in, 0.0).astype(jnp.bfloat16)
        old = g
        g = result.astype(jnp.float32)
        out_ref[s, :, 0:tile_rows, :] = (
            g[:, HALO : HALO + out_pairs].reshape(bins, tile_rows, LANES).astype(jnp.bfloat16)
        )
        g3c = g3.astype(jnp.float32)[:, centre].astype(jnp.bfloat16)
        hc = h.astype(jnp.float32)[:, centre].astype(jnp.bfloat16)
        xc = xx.astype(jnp.float32)[:, centre].astype(jnp.bfloat16)
        gc = jnp.concatenate([v[:, centre] for v in gg], axis=3).astype(jnp.bfloat16)
        dt = mm(flat(hc), flat(g3c), ((0,), (0,)))
        d = mm(flat(xc), flat(gc), ((0,), (0,)))

        def block(a, r, i, b):
            at = i * LANES + b * chans
            return a[r * chans : (r + 1) * chans, at : at + chans]

        taps = []
        for i in range(3):
            taps.append(block(d, 0, i, 1) + block(d, 3, i, 0))
            taps.append(block(d, 0, i, 0) + block(d, 1, i, 1))
            taps.append(block(d, 1, i, 0) + block(d, 2, i, 1))
        for k in range(3):
            taps.append(block(dt, 0, k, 0) + block(dt, 1, k, 1))
        for k in range(6):
            ds[k * chans : (k + 1) * chans, :] = jnp.concatenate(
                [taps[2 * k], taps[2 * k + 1]], axis=1
            )
        for n in range(bins):
            got = piece * n
            rows = 6 * chans // bins
            out_ref[s, n, tile_rows : tile_rows + rows, :] = ds[
                rows * n : rows * (n + 1), :
            ].astype(jnp.bfloat16)


def pack(a, tm, tiles, pairs):
    micro, local, rows, width = a.shape
    frame = width // LANES
    a = jnp.pad(a, ((0, 0), (0, 0), (0, ROWS - rows), (0, 0)))
    a = a.reshape(micro * local, ROWS, frame, LANES).transpose(0, 2, 1, 3)
    a = jnp.pad(a, ((0, 0), (HALO, pairs), (0, 0), (0, 0)))
    cut = [a[:, tiles * m : tiles * m + pairs] for m in range(tm)]
    return jnp.stack(cut, axis=1).reshape(micro * local * tm, pairs * ROWS, LANES)


def body(acts, cot, spatial_weight, temporal_weight):
    sections, tm = lax.axis_size("section"), lax.axis_size("tm")
    both = ("section", "tm")
    micro, local, rows, width = cot.shape
    chans = spatial_weight.shape[-1]
    frame = width // LANES
    tiles = frame // tm
    pairs = tiles + 2 * HALO
    pairs += pairs % 2
    ext = pairs * ROWS
    share = -(-ext // (16 * sections)) * 16
    weights = lax.all_gather(
        jnp.concatenate([spatial_weight[0], temporal_weight[0]]), "section", axis=0
    )
    mine = pack(acts[0], tm, tiles, pairs)
    top = pack(cot, tm, tiles, pairs)
    top = jnp.pad(top, ((0, 0), (0, share * sections - ext), (0, 0)))
    top = lax.dynamic_slice_in_dim(top, lax.axis_index("section") * share, share, 1)
    message = jnp.concatenate([mine, top], axis=1)
    got = lax.all_to_all(message, both, 0, 0, tiled=True)
    got = got.reshape(sections, tm, ext + share, LANES)
    tile_rows = tiles * ROWS + (tiles * ROWS) % 16
    piece = 6 * chans // tm
    out = pl.pallas_call(
        functools.partial(kernel, tiles, frame),
        out_shape=jax.ShapeDtypeStruct((sections, tm, tile_rows + piece, LANES), jnp.bfloat16),
        in_specs=[pl.BlockSpec(memory_space=pltpu.VMEM)] * 2,
        out_specs=pl.BlockSpec(memory_space=pltpu.VMEM),
        scratch_shapes=[
            pltpu.VMEM((1, pairs, ROWS, LANES), jnp.float32),
            pltpu.VMEM((6 * chans, LANES), jnp.float32),
        ],
        compiler_params=pltpu.CompilerParams(vmem_limit_bytes=48 * 2**20),
    )(got, weights)
    home = lax.all_to_all(
        out.reshape(sections * tm, tile_rows + piece, LANES), both, 0, 0, tiled=True
    )
    grad = home[:, : tiles * ROWS].reshape(micro, local, tm * tiles, ROWS, LANES)
    grad = grad.transpose(0, 1, 3, 2, 4)[:, :, :rows].reshape(micro, local, rows, width)
    partial = jnp.sum(home[:, tile_rows:].astype(jnp.float32), axis=0)
    full = jnp.sum(lax.all_gather(partial, ("tm", "batch"), axis=0).reshape(tm, -1, piece, LANES), axis=1)
    full = full.reshape(6, chans, 2, chans).transpose(0, 2, 1, 3).reshape(12, chans, chans)
    return grad[None], full[None, :9], full[None, 9:]


def solution(mesh):
    in_specs = (
        P("section", "batch", "tm", None, None),
        P("batch", "tm", None, None),
        P("section", None, None, None),
        P("section", None, None, None),
    )
    out_specs = (
        P("section", "batch", "tm", None, None),
        P("section", None, None, None),
        P("section", None, None, None),
    )
    return jax.shard_map(body, mesh=mesh, in_specs=in_specs, out_specs=out_specs, check_vma=False)
```

```python
import functools

import jax
import jax.numpy as jnp
from jax import lax
from jax.experimental import pallas as pl
from jax.experimental.pallas import tpu as pltpu
from jax.sharding import PartitionSpec as P

DILATION = 2
ROWS = 8
LANES = 128
HALO = 3
MESH = pl.DeviceIdType.MESH


def neighbours(x):
    none = jnp.zeros_like(x[:, :1])
    after = jnp.concatenate([x[:, 1:], none], axis=1)
    before = jnp.concatenate([none, x[:, :-1]], axis=1)
    lane = lax.broadcasted_iota(jnp.int32, x.shape, 3)
    return jnp.where(lane < LANES // 2, after, before)


def flat(x):
    return x.reshape(-1, x.shape[-1])


def mm(a, b, dims):
    return lax.dot_general(a, b, (dims, ((), ())), preferred_element_type=jnp.float32)


def taps_of(d, dt, chans):
    def block(a, r, i, b):
        at = i * LANES + b * chans
        return a[r * chans : (r + 1) * chans, at : at + chans]

    taps = []
    for i in range(3):
        taps.append(block(d, 0, i, 1) + block(d, 3, i, 0))
        taps.append(block(d, 0, i, 0) + block(d, 1, i, 1))
        taps.append(block(d, 1, i, 0) + block(d, 2, i, 1))
    for k in range(3):
        taps.append(block(dt, 0, k, 0) + block(dt, 1, k, 1))
    return taps


def set_weights(ws_ref, wt_ref, fwd, back, time):
    chans = ws_ref.shape[-1]
    zero = jnp.zeros((chans, chans), jnp.bfloat16)
    for i in range(3):
        a, b, c = [ws_ref[3 * i + j] for j in range(3)]
        at = slice(i * LANES, (i + 1) * LANES)
        rows = [[b, a], [c, b], [zero, c], [a, zero]]
        fwd[:, at] = jnp.concatenate([jnp.concatenate(v, axis=1) for v in rows], axis=0)
        at = slice(i * 2 * LANES, (i + 1) * 2 * LANES)
        rows = [[b, a, zero, c], [c, b, a, zero]]
        back[:, at] = jnp.concatenate([jnp.concatenate(v, axis=1) for v in rows], axis=0)
        at = slice(i * LANES, (i + 1) * LANES)
        rows = [[wt_ref[i], zero], [zero, wt_ref[i]]]
        time[:, at] = jnp.concatenate([jnp.concatenate(v, axis=1) for v in rows], axis=0)


def pack(frame, stage, c, tiles):
    tm, pairs = stage.shape[0], stage.shape[2] // ROWS
    rows, width = frame.shape
    v = frame.astype(jnp.float32)
    v = jnp.concatenate([v, jnp.zeros((ROWS - rows, width), jnp.float32)], axis=0)
    zero = jnp.zeros((1, ROWS, LANES), jnp.float32)
    cut = [v[:, LANES * p : LANES * (p + 1)][None] for p in range(width // LANES)]
    cut = [zero] * HALO + cut + [zero] * pairs
    for m in range(tm):
        part = jnp.concatenate(cut[tiles * m : tiles * m + pairs], axis=0)
        stage[m, c] = part.reshape(pairs * ROWS, LANES).astype(jnp.bfloat16)


def kernel(
    sections, batches, tiles, acts, cot, ws_ref, wt_ref, out, grads,
    x_stage, g_stage, x_buf, g_buf, r_buf, o_buf, home, fwd, back, time, acc, acc_t, ds,
    w_send, w_recv, w_piece, w_full,
    x_sem, g_sem, z_sem, o_sem, w_sem, f_sem,
):
    tm = x_stage.shape[0]
    chains, frame_rows, width = acts.shape
    chans = ws_ref.shape[-1]
    ext = x_buf.shape[2]
    pairs = ext // ROWS
    tile_rows = o_buf.shape[2]
    out_pairs = tile_rows // ROWS
    group = tm * batches
    section, me, core = [lax.axis_index(a) for a in ("section", "tm", "batch")]
    rank = me * batches + core

    def member(e):
        other = lax.rem(rank + e, group)
        return other, (section, other // batches, lax.rem(other, batches))

    def peer(d):
        other = lax.rem(me + d, tm)
        return other, (section, other, core)

    barrier = pltpu.get_barrier_semaphore()
    for e in range(1, group):
        pl.semaphore_signal(barrier, inc=1, device_id=member(e)[1], device_id_type=MESH)

    @pl.when(section > 0)
    def _():
        pl.semaphore_signal(barrier, inc=1, device_id=(section - 1, me, core), device_id_type=MESH)

    @pl.when(section < sections - 1)
    def _():
        pl.semaphore_signal(barrier, inc=1, device_id=(section + 1, me, core), device_id_type=MESH)

    def copy(src, dst, sems, at, device):
        return pltpu.make_async_remote_copy(
            src_ref=src, dst_ref=dst, send_sem=sems.at[(0,) + at], recv_sem=sems.at[(1,) + at],
            device_id=device, device_id_type=MESH,
        )

    def x_copy(c, d):
        other, device = peer(d)
        return copy(x_stage.at[other, c], x_buf.at[c, me], x_sem, (c, d - 1), device)

    def g_copy(c, d):
        other, device = peer(d)
        return copy(g_stage.at[other, c], g_buf.at[c, me], g_sem, (c, d - 1), device)

    def z_copy(c):
        return copy(r_buf.at[c], g_buf.at[c], z_sem, (c,), (lax.max(section - 1, 0), me, core))

    def o_copy(c, d):
        other, device = peer(d)
        return copy(o_buf.at[c, other], home.at[c, me], o_sem, (c, d - 1), device)

    def w_copy(e):
        other, device = member(e)
        return copy(w_send.at[other], w_recv.at[rank], w_sem, (e - 1,), device)

    def f_copy(e):
        return copy(w_piece, w_full.at[rank], f_sem, (e - 1,), member(e)[1])

    pack(acts[0], x_stage, 0, tiles)

    @pl.when(section == sections - 1)
    def _():
        pack(cot[0], g_stage, 0, tiles)

    more = (section > 0).astype(jnp.int32) + (section < sections - 1).astype(jnp.int32)
    pl.semaphore_wait(barrier, group - 1 + more)

    def send(c, carry):
        @pl.when(c > 0)
        def _():
            pack(acts[c], x_stage, c, tiles)

            @pl.when(section == sections - 1)
            def _():
                pack(cot[c], g_stage, c, tiles)

        for d in range(1, tm):
            x_copy(c, d).start()
        x_buf[c, me] = x_stage[me, c]

        @pl.when(section == sections - 1)
        def _():
            for d in range(1, tm):
                g_copy(c, d).start()
            g_buf[c, me] = g_stage[me, c]

        return carry

    lax.fori_loop(0, chains, send, 0)
    set_weights(ws_ref, wt_ref, fwd, back, time)
    acc[...] = jnp.zeros_like(acc)
    acc_t[...] = jnp.zeros_like(acc_t)

    shape = (tm, pairs, ROWS, LANES)
    blank = jnp.zeros((1, pairs, ROWS, LANES), jnp.float32)
    centre = slice(HALO, HALO + tiles)

    def turn(c, carry):
        for d in range(1, tm):
            x_copy(c, d).wait_recv()
        x = x_buf[c].astype(jnp.float32).reshape(shape)
        xx = jnp.concatenate([x, neighbours(x)], axis=3)
        y = mm(flat(xx).astype(jnp.bfloat16), fwd[...], ((1,), (0,)))
        part = [y[:, LANES * i : LANES * (i + 1)].reshape(-1, ROWS, LANES) for i in range(3)]
        z = part[1] + pltpu.roll(part[0], 1, 1) + pltpu.roll(part[2], ROWS - 1, 1)
        z = z.reshape(shape)
        sig = jax.nn.sigmoid(z)
        h = z * sig
        slope = sig * (1.0 + z * (1.0 - sig))

        @pl.when(section == sections - 1)
        def _():
            for d in range(1, tm):
                g_copy(c, d).wait_recv()

        @pl.when(section < sections - 1)
        def _():
            z_copy(c).wait_recv()

        g = g_buf[c].astype(jnp.float32).reshape(shape)
        g3 = jnp.concatenate(
            [
                jnp.concatenate([g[1:], blank], axis=0),
                g,
                jnp.concatenate([blank, g[:-1]], axis=0),
            ],
            axis=3,
        )
        gh = mm(flat(g3).astype(jnp.bfloat16), time[...], ((1,), (1,))).astype(jnp.bfloat16)
        gz = (gh.astype(jnp.float32).reshape(shape) * slope).astype(jnp.bfloat16)
        gz = gz.astype(jnp.float32)
        flat_gz = gz.reshape(-1, ROWS, LANES)
        gg = [
            pltpu.roll(flat_gz, ROWS - 1, 1).reshape(shape),
            gz,
            pltpu.roll(flat_gz, 1, 1).reshape(shape),
        ]
        sides = []
        for v in gg:
            sides += [v, neighbours(v)]
        sides = jnp.concatenate(sides, axis=3).astype(jnp.bfloat16)
        inner = mm(flat(sides), back[...], ((1,), (1,))).reshape(shape)
        place = me * tiles - HALO + lax.broadcasted_iota(jnp.int32, shape, 1)
        row = lax.broadcasted_iota(jnp.int32, shape, 2)
        inside = (place >= 0) & (place < width // LANES) & (row < frame_rows)
        result = jnp.where(inside, g + inner, 0.0)
        r_buf[c] = result.reshape(tm, ext, LANES).astype(jnp.bfloat16)

        @pl.when(section > 0)
        def _():
            z_copy(c).start()

        o_buf[c] = (
            result[:, HALO : HALO + out_pairs].reshape(tm, tile_rows, LANES).astype(jnp.bfloat16)
        )
        for d in range(1, tm):
            o_copy(c, d).start()
        home[c, me] = o_buf[c, me]
        hc = flat(h[:, centre]).astype(jnp.bfloat16)
        acc_t[...] += mm(hc, flat(g3[:, centre]).astype(jnp.bfloat16), ((0,), (0,)))
        gc = jnp.concatenate([v[:, centre] for v in gg], axis=3).astype(jnp.bfloat16)
        acc[...] += mm(flat(xx[:, centre]).astype(jnp.bfloat16), flat(gc), ((0,), (0,)))
        return carry

    lax.fori_loop(0, chains, turn, 0)

    taps = taps_of(acc[...], acc_t[...], chans)
    for k in range(6):
        ds[k * chans : (k + 1) * chans, :] = jnp.concatenate([taps[2 * k], taps[2 * k + 1]], axis=1)
    rows = w_send.shape[1]
    for k in range(group):
        w_send[k] = ds[k * rows : (k + 1) * rows, :].astype(jnp.bfloat16)
    for e in range(1, group):
        w_copy(e).start()
    w_recv[rank] = w_send[rank]

    def unpack(c, carry):
        for d in range(1, tm):
            o_copy(c, d).wait_recv()
        v = home[c].astype(jnp.float32).reshape(tm, out_pairs, ROWS, LANES)
        cut = [v[m, p] for m in range(tm) for p in range(tiles)]
        out[c] = jnp.concatenate(cut, axis=1)[:frame_rows].astype(jnp.bfloat16)
        return carry

    lax.fori_loop(0, chains - 1, unpack, 0)
    for e in range(1, group):
        w_copy(e).wait_recv()
    w_piece[...] = jnp.sum(w_recv[...].astype(jnp.float32), axis=0)
    for e in range(1, group):
        f_copy(e).start()
    w_full[rank] = w_piece[...]
    unpack(chains - 1, 0)

    for e in range(1, group):
        f_copy(e).wait_recv()
    for k in range(group):
        ds[k * rows : (k + 1) * rows, :] = w_full[k]
    for t in range(12):
        both = ds[(t // 2) * chans : (t // 2 + 1) * chans, :]
        grads[t] = both[:, (t % 2) * chans : (t % 2 + 1) * chans]

    def finish(c, carry):
        for d in range(1, tm):
            x_copy(c, d).wait_send()
            o_copy(c, d).wait_send()

        @pl.when(section == sections - 1)
        def _():
            for d in range(1, tm):
                g_copy(c, d).wait_send()

        @pl.when(section > 0)
        def _():
            z_copy(c).wait_send()

        return carry

    lax.fori_loop(0, chains, finish, 0)
    for e in range(1, group):
        w_copy(e).wait_send()
        f_copy(e).wait_send()


def body(acts, cot, spatial_weight, temporal_weight):
    sections, tm, batches = [lax.axis_size(a) for a in ("section", "tm", "batch")]
    micro, local, rows, width = cot.shape
    chans = spatial_weight.shape[-1]
    chains = micro * local
    group = tm * batches
    tiles = width // LANES // tm
    pairs = tiles + 2 * HALO
    pairs += pairs % 2
    ext = pairs * ROWS
    tile_rows = tiles * ROWS + (tiles * ROWS) % 16
    piece = 6 * chans // group
    bf16, f32 = jnp.bfloat16, jnp.float32
    vmem, dma = pltpu.VMEM, pltpu.SemaphoreType.DMA
    grad, kernels = pl.pallas_call(
        functools.partial(kernel, sections, batches, tiles),
        out_shape=[
            jax.ShapeDtypeStruct((chains, rows, width), bf16),
            jax.ShapeDtypeStruct((12, chans, chans), f32),
        ],
        in_specs=[pl.BlockSpec(memory_space=vmem)] * 4,
        out_specs=[pl.BlockSpec(memory_space=vmem)] * 2,
        scratch_shapes=[
            vmem((tm, chains, ext, LANES), bf16),
            vmem((tm, chains, ext, LANES), bf16),
            vmem((chains, tm, ext, LANES), bf16),
            vmem((chains, tm, ext, LANES), bf16),
            vmem((chains, tm, ext, LANES), bf16),
            vmem((chains, tm, tile_rows, LANES), bf16),
            vmem((chains, tm, tile_rows, LANES), bf16),
            vmem((2 * LANES, 3 * LANES), bf16),
            vmem((LANES, 6 * LANES), bf16),
            vmem((LANES, 3 * LANES), bf16),
            vmem((2 * LANES, 3 * LANES), f32),
            vmem((LANES, 3 * LANES), f32),
            vmem((6 * chans, LANES), f32),
            vmem((group, piece, LANES), bf16),
            vmem((group, piece, LANES), bf16),
            vmem((piece, LANES), f32),
            vmem((group, piece, LANES), f32),
            dma((2, chains, tm - 1)),
            dma((2, chains, tm - 1)),
            dma((2, chains)),
            dma((2, chains, tm - 1)),
            dma((2, group - 1)),
            dma((2, group - 1)),
        ],
        compiler_params=pltpu.CompilerParams(
            collective_id=0, has_side_effects=True, vmem_limit_bytes=56 * 2**20
        ),
    )(acts.reshape(chains, rows, width), cot.reshape(chains, rows, width), spatial_weight[0], temporal_weight[0])
    return grad.reshape(acts.shape), kernels[None, :9], kernels[None, 9:]


def solution(mesh):
    in_specs = (
        P("section", "batch", "tm", None, None),
        P("batch", "tm", None, None),
        P("section", None, None, None),
        P("section", None, None, None),
    )
    out_specs = (
        P("section", "batch", "tm", None, None),
        P("section", None, None, None),
        P("section", None, None, None),
    )
    return jax.shard_map(body, mesh=mesh, in_specs=in_specs, out_specs=out_specs, check_vma=False)
```

```python
import functools

import jax
import jax.numpy as jnp
from jax import lax
from jax.experimental import pallas as pl
from jax.experimental.pallas import tpu as pltpu
from jax.sharding import PartitionSpec as P

DILATION = 2
ROWS = 8
LANES = 128
HALO = 3
MESH = pl.DeviceIdType.MESH


def neighbours(x):
    none = jnp.zeros_like(x[:, :1])
    after = jnp.concatenate([x[:, 1:], none], axis=1)
    before = jnp.concatenate([none, x[:, :-1]], axis=1)
    lane = lax.broadcasted_iota(jnp.int32, x.shape, 3)
    return jnp.where(lane < LANES // 2, after, before)


def flat(x):
    return x.reshape(-1, x.shape[-1])


def mm(a, b, dims):
    return lax.dot_general(a, b, (dims, ((), ())), preferred_element_type=jnp.float32)


def taps_of(d, dt, chans):
    def block(a, r, i, b):
        at = i * LANES + b * chans
        return a[r * chans : (r + 1) * chans, at : at + chans]

    taps = []
    for i in range(3):
        taps.append(block(d, 0, i, 1) + block(d, 3, i, 0))
        taps.append(block(d, 0, i, 0) + block(d, 1, i, 1))
        taps.append(block(d, 1, i, 0) + block(d, 2, i, 1))
    for k in range(3):
        taps.append(block(dt, 0, k, 0) + block(dt, 1, k, 1))
    return taps


def set_weights(ws_ref, wt_ref, fwd, back, time):
    chans = ws_ref.shape[-1]
    zero = jnp.zeros((chans, chans), jnp.bfloat16)
    for i in range(3):
        a, b, c = [ws_ref[3 * i + j] for j in range(3)]
        at = slice(i * LANES, (i + 1) * LANES)
        rows = [[b, a], [c, b], [zero, c], [a, zero]]
        fwd[:, at] = jnp.concatenate([jnp.concatenate(v, axis=1) for v in rows], axis=0)
        at = slice(i * 2 * LANES, (i + 1) * 2 * LANES)
        rows = [[b, a, zero, c], [c, b, a, zero]]
        back[:, at] = jnp.concatenate([jnp.concatenate(v, axis=1) for v in rows], axis=0)
        at = slice(i * LANES, (i + 1) * LANES)
        rows = [[wt_ref[i], zero], [zero, wt_ref[i]]]
        time[:, at] = jnp.concatenate([jnp.concatenate(v, axis=1) for v in rows], axis=0)


def pack(frame, stage, c, tiles, line, skip):
    tm, size = stage.shape[0], stage.shape[2]
    rows, width = frame.shape
    v = frame.astype(jnp.float32)
    for p in range(width // LANES):
        at = (p + HALO) * rows
        line[at : at + rows, :] = v[:, LANES * p : LANES * (p + 1)]
    for m in range(tm):
        at = (tiles * m + skip) * rows
        stage[m, c] = line[at : at + size, :].astype(jnp.bfloat16)


def spread(packed, loose, wide, rows, first, count):
    loose[...] = packed.astype(jnp.float32)
    for n in range(loose.shape[0]):
        for p in range(count):
            wide[n, first + p, 0:rows, :] = loose[n, rows * p : rows * (p + 1), :]


def kernel(
    sections, batches, tiles, acts, cot, ws_ref, wt_ref, out, spatial, temporal,
    x_stage, g_stage, x_buf, g_buf, r_buf, o_buf, home, fwd, back, time, acc, acc_t, ds,
    w_send, w_recv, w_piece, w_full,
    line, x_loose, g_loose, o_loose, x_wide, g_wide,
    x_sem, g_sem, z_sem, o_sem, w_sem, f_sem,
):
    tm = x_stage.shape[0]
    chains, frame_rows, width = acts.shape
    chans = ws_ref.shape[-1]
    pairs = x_wide.shape[1]
    tile_rows = o_buf.shape[2]
    group = tm * batches
    section, me, core = [lax.axis_index(a) for a in ("section", "tm", "batch")]
    rank = me * batches + core

    def member(e):
        other = lax.rem(rank + e, group)
        return other, (section, other // batches, lax.rem(other, batches))

    def peer(d):
        other = lax.rem(me + d, tm)
        return other, (section, other, core)

    barrier = pltpu.get_barrier_semaphore()
    for e in range(1, group):
        pl.semaphore_signal(barrier, inc=1, device_id=member(e)[1], device_id_type=MESH)

    @pl.when(section > 0)
    def _():
        pl.semaphore_signal(barrier, inc=1, device_id=(section - 1, me, core), device_id_type=MESH)

    @pl.when(section < sections - 1)
    def _():
        pl.semaphore_signal(barrier, inc=1, device_id=(section + 1, me, core), device_id_type=MESH)

    def copy(src, dst, sems, at, device):
        return pltpu.make_async_remote_copy(
            src_ref=src, dst_ref=dst, send_sem=sems.at[(0,) + at], recv_sem=sems.at[(1,) + at],
            device_id=device, device_id_type=MESH,
        )

    def x_copy(c, d):
        other, device = peer(d)
        return copy(x_stage.at[other, c], x_buf.at[c, me], x_sem, (c, d - 1), device)

    def g_copy(c, d):
        other, device = peer(d)
        return copy(g_stage.at[other, c], g_buf.at[c, me], g_sem, (c, d - 1), device)

    def z_copy(c):
        return copy(r_buf.at[c], g_buf.at[c], z_sem, (c,), (lax.max(section - 1, 0), me, core))

    def o_copy(c, d):
        other, device = peer(d)
        return copy(o_buf.at[c, other], home.at[c, me], o_sem, (c, d - 1), device)

    def w_copy(e):
        other, device = member(e)
        return copy(w_send.at[other], w_recv.at[rank], w_sem, (e - 1,), device)

    def f_copy(e):
        return copy(w_piece, w_full.at[rank], f_sem, (e - 1,), member(e)[1])

    line[...] = jnp.zeros_like(line)
    x_wide[...] = jnp.zeros_like(x_wide)
    g_wide[...] = jnp.zeros_like(g_wide)
    g_loose[...] = jnp.zeros_like(g_loose)
    pack(acts[0], x_stage, 0, tiles, line, 0)

    @pl.when(section == sections - 1)
    def _():
        pack(cot[0], g_stage, 0, tiles, line, 1)

    more = (section > 0).astype(jnp.int32) + (section < sections - 1).astype(jnp.int32)
    pl.semaphore_wait(barrier, group - 1 + more)

    def send(c, carry):
        @pl.when(c > 0)
        def _():
            pack(acts[c], x_stage, c, tiles, line, 0)

            @pl.when(section == sections - 1)
            def _():
                pack(cot[c], g_stage, c, tiles, line, 1)

        for d in range(1, tm):
            x_copy(c, d).start()
        x_buf[c, me] = x_stage[me, c]

        @pl.when(section == sections - 1)
        def _():
            for d in range(1, tm):
                g_copy(c, d).start()
            g_buf[c, me] = g_stage[me, c]

        return carry

    lax.fori_loop(0, chains, send, 0)
    set_weights(ws_ref, wt_ref, fwd, back, time)
    acc[...] = jnp.zeros_like(acc)
    acc_t[...] = jnp.zeros_like(acc_t)

    shape = (tm, pairs, ROWS, LANES)
    blank = jnp.zeros((1, pairs, ROWS, LANES), jnp.float32)
    centre = slice(HALO, HALO + tiles)

    def turn(c, carry):
        for d in range(1, tm):
            x_copy(c, d).wait_recv()
        spread(x_buf[c], x_loose, x_wide, frame_rows, 0, pairs)
        x = x_wide[...]
        xx = jnp.concatenate([x, neighbours(x)], axis=3)
        y = mm(flat(xx).astype(jnp.bfloat16), fwd[...], ((1,), (0,)))
        part = [y[:, LANES * i : LANES * (i + 1)].reshape(-1, ROWS, LANES) for i in range(3)]
        z = part[1] + pltpu.roll(part[0], 1, 1) + pltpu.roll(part[2], ROWS - 1, 1)
        z = z.reshape(shape)
        sig = jax.nn.sigmoid(z)
        h = z * sig
        slope = sig * (1.0 + z * (1.0 - sig))

        @pl.when(section == sections - 1)
        def _():
            for d in range(1, tm):
                g_copy(c, d).wait_recv()

        @pl.when(section < sections - 1)
        def _():
            z_copy(c).wait_recv()

        spread(g_buf[c], g_loose, g_wide, frame_rows, 1, pairs - 2)
        g = g_wide[...]
        g3 = jnp.concatenate(
            [
                jnp.concatenate([g[1:], blank], axis=0),
                g,
                jnp.concatenate([blank, g[:-1]], axis=0),
            ],
            axis=3,
        )
        gh = mm(flat(g3).astype(jnp.bfloat16), time[...], ((1,), (1,))).astype(jnp.bfloat16)
        gz = (gh.astype(jnp.float32).reshape(shape) * slope).astype(jnp.bfloat16)
        gz = gz.astype(jnp.float32)
        flat_gz = gz.reshape(-1, ROWS, LANES)
        gg = [
            pltpu.roll(flat_gz, ROWS - 1, 1).reshape(shape),
            gz,
            pltpu.roll(flat_gz, 1, 1).reshape(shape),
        ]
        sides = []
        for v in gg:
            sides += [v, neighbours(v)]
        sides = jnp.concatenate(sides, axis=3).astype(jnp.bfloat16)
        inner = mm(flat(sides), back[...], ((1,), (1,))).reshape(shape)
        place = me * tiles - HALO + lax.broadcasted_iota(jnp.int32, shape, 1)
        row = lax.broadcasted_iota(jnp.int32, shape, 2)
        inside = (place >= 0) & (place < width // LANES) & (row < frame_rows)
        result = jnp.where(inside, g + inner, 0.0)
        for n in range(tm):
            for p in range(pairs - 2):
                at = frame_rows * p
                g_loose[n, at : at + frame_rows, :] = result[n, p + 1, 0:frame_rows]
        r_buf[c] = g_loose[...].astype(jnp.bfloat16)

        @pl.when(section > 0)
        def _():
            z_copy(c).start()

        at = (HALO - 1) * frame_rows
        o_buf[c] = g_loose[:, at : at + tile_rows, :].astype(jnp.bfloat16)
        for d in range(1, tm):
            o_copy(c, d).start()
        home[c, me] = o_buf[c, me]
        hc = flat(h[:, centre]).astype(jnp.bfloat16)
        acc_t[...] += mm(hc, flat(g3[:, centre]).astype(jnp.bfloat16), ((0,), (0,)))
        gc = jnp.concatenate([v[:, centre] for v in gg], axis=3).astype(jnp.bfloat16)
        acc[...] += mm(flat(xx[:, centre]).astype(jnp.bfloat16), flat(gc), ((0,), (0,)))
        return carry

    lax.fori_loop(0, chains, turn, 0)

    taps = taps_of(acc[...], acc_t[...], chans)
    for k in range(6):
        ds[k * chans : (k + 1) * chans, :] = jnp.concatenate([taps[2 * k], taps[2 * k + 1]], axis=1)
    rows = w_send.shape[1]
    for k in range(group):
        w_send[k] = ds[k * rows : (k + 1) * rows, :].astype(jnp.bfloat16)
    for e in range(1, group):
        w_copy(e).start()
    w_recv[rank] = w_send[rank]

    def unpack(c, carry):
        for d in range(1, tm):
            o_copy(c, d).wait_recv()
        o_loose[...] = home[c].astype(jnp.float32)
        cut = [
            o_loose[m, frame_rows * p : frame_rows * (p + 1), :]
            for m in range(tm)
            for p in range(tiles)
        ]
        out[c] = jnp.concatenate(cut, axis=1).astype(jnp.bfloat16)
        return carry

    lax.fori_loop(0, chains - 1, unpack, 0)
    for e in range(1, group):
        w_copy(e).wait_recv()
    w_piece[...] = jnp.sum(w_recv[...].astype(jnp.float32), axis=0)
    for e in range(1, group):
        f_copy(e).start()
    w_full[rank] = w_piece[...]
    unpack(chains - 1, 0)

    for e in range(1, group):
        f_copy(e).wait_recv()
    for k in range(group):
        ds[k * rows : (k + 1) * rows, :] = w_full[k]
    for t in range(12):
        both = ds[(t // 2) * chans : (t // 2 + 1) * chans, :]
        half = both[:, (t % 2) * chans : (t % 2 + 1) * chans]
        if t < 9:
            spatial[t] = half
        else:
            temporal[t - 9] = half

    def finish(c, carry):
        for d in range(1, tm):
            x_copy(c, d).wait_send()
            o_copy(c, d).wait_send()

        @pl.when(section == sections - 1)
        def _():
            for d in range(1, tm):
                g_copy(c, d).wait_send()

        @pl.when(section > 0)
        def _():
            z_copy(c).wait_send()

        return carry

    lax.fori_loop(0, chains, finish, 0)
    for e in range(1, group):
        w_copy(e).wait_send()
        f_copy(e).wait_send()


def body(acts, cot, spatial_weight, temporal_weight):
    sections, tm, batches = [lax.axis_size(a) for a in ("section", "tm", "batch")]
    micro, local, rows, width = cot.shape
    chans = spatial_weight.shape[-1]
    chains = micro * local
    group = tm * batches
    tiles = width // LANES // tm
    pairs = tiles + 2 * HALO
    pairs += pairs % 2
    x_rows, g_rows, tile_rows = [-(-n * rows // 16) * 16 for n in (pairs, pairs - 2, tiles)]
    piece = 6 * chans // group
    bf16, f32 = jnp.bfloat16, jnp.float32
    vmem, dma = pltpu.VMEM, pltpu.SemaphoreType.DMA
    grad, spatial, temporal = pl.pallas_call(
        functools.partial(kernel, sections, batches, tiles),
        out_shape=[
            jax.ShapeDtypeStruct((chains, rows, width), bf16),
            jax.ShapeDtypeStruct((9, chans, chans), f32),
            jax.ShapeDtypeStruct((3, chans, chans), f32),
        ],
        in_specs=[pl.BlockSpec(memory_space=vmem)] * 4,
        out_specs=[pl.BlockSpec(memory_space=vmem)] * 3,
        scratch_shapes=[
            vmem((tm, chains, x_rows, LANES), bf16),
            vmem((tm, chains, g_rows, LANES), bf16),
            vmem((chains, tm, x_rows, LANES), bf16),
            vmem((chains, tm, g_rows, LANES), bf16),
            vmem((chains, tm, g_rows, LANES), bf16),
            vmem((chains, tm, tile_rows, LANES), bf16),
            vmem((chains, tm, tile_rows, LANES), bf16),
            vmem((2 * LANES, 3 * LANES), bf16),
            vmem((LANES, 6 * LANES), bf16),
            vmem((LANES, 3 * LANES), bf16),
            vmem((2 * LANES, 3 * LANES), f32),
            vmem((LANES, 3 * LANES), f32),
            vmem((6 * chans, LANES), f32),
            vmem((group, piece, LANES), bf16),
            vmem((group, piece, LANES), bf16),
            vmem((piece, LANES), f32),
            vmem((group, piece, LANES), f32),
            vmem(((width // LANES + HALO + pairs) * rows + 16, LANES), f32),
            vmem((tm, x_rows, LANES), f32),
            vmem((tm, g_rows, LANES), f32),
            vmem((tm, tile_rows, LANES), f32),
            vmem((tm, pairs, ROWS, LANES), f32),
            vmem((tm, pairs, ROWS, LANES), f32),
            dma((2, chains, tm - 1)),
            dma((2, chains, tm - 1)),
            dma((2, chains)),
            dma((2, chains, tm - 1)),
            dma((2, group - 1)),
            dma((2, group - 1)),
        ],
        compiler_params=pltpu.CompilerParams(
            collective_id=0, has_side_effects=True, vmem_limit_bytes=56 * 2**20
        ),
    )(acts.reshape(chains, rows, width), cot.reshape(chains, rows, width), spatial_weight[0], temporal_weight[0])
    return grad.reshape(acts.shape), spatial[None], temporal[None]


def solution(mesh):
    in_specs = (
        P("section", "batch", "tm", None, None),
        P("batch", "tm", None, None),
        P("section", None, None, None),
        P("section", None, None, None),
    )
    out_specs = (
        P("section", "batch", "tm", None, None),
        P("section", None, None, None),
        P("section", None, None, None),
    )
    return jax.shard_map(body, mesh=mesh, in_specs=in_specs, out_specs=out_specs, check_vma=False)
```

```python
import functools

import jax
import jax.numpy as jnp
from jax import lax
from jax.experimental import pallas as pl
from jax.experimental.pallas import tpu as pltpu
from jax.sharding import PartitionSpec as P

DILATION = 2
ROWS = 8
LANES = 128
HALO = 3
MESH = pl.DeviceIdType.MESH


def neighbours(x):
    none = jnp.zeros_like(x[:, :1])
    after = jnp.concatenate([x[:, 1:], none], axis=1)
    before = jnp.concatenate([none, x[:, :-1]], axis=1)
    lane = lax.broadcasted_iota(jnp.int32, x.shape, 3)
    return jnp.where(lane < LANES // 2, after, before)


def flat(x):
    return x.reshape(-1, x.shape[-1])


def mm(a, b, dims):
    return lax.dot_general(a, b, (dims, ((), ())), preferred_element_type=jnp.float32)


def taps_of(d, dt, chans):
    def block(a, r, i, b):
        at = i * LANES + b * chans
        return a[r * chans : (r + 1) * chans, at : at + chans]

    taps = []
    for i in range(3):
        taps.append(block(d, 0, i, 1) + block(d, 3, i, 0))
        taps.append(block(d, 0, i, 0) + block(d, 1, i, 1))
        taps.append(block(d, 1, i, 0) + block(d, 2, i, 1))
    for k in range(3):
        taps.append(block(dt, 0, k, 0) + block(dt, 1, k, 1))
    return taps


def set_weights(ws_ref, wt_ref, fwd, back, time):
    chans = ws_ref.shape[-1]
    zero = jnp.zeros((chans, chans), jnp.bfloat16)
    for i in range(3):
        a, b, c = [ws_ref[3 * i + j] for j in range(3)]
        at = slice(i * LANES, (i + 1) * LANES)
        rows = [[b, a], [c, b], [zero, c], [a, zero]]
        fwd[:, at] = jnp.concatenate([jnp.concatenate(v, axis=1) for v in rows], axis=0)
        at = slice(i * 2 * LANES, (i + 1) * 2 * LANES)
        rows = [[b, a, zero, c], [c, b, a, zero]]
        back[:, at] = jnp.concatenate([jnp.concatenate(v, axis=1) for v in rows], axis=0)
        at = slice(i * LANES, (i + 1) * LANES)
        rows = [[wt_ref[i], zero], [zero, wt_ref[i]]]
        time[:, at] = jnp.concatenate([jnp.concatenate(v, axis=1) for v in rows], axis=0)


def pack(frame, stage, c, tiles, line, skip):
    tm, size = stage.shape[0], stage.shape[2]
    rows, width = frame.shape
    v = frame.astype(jnp.float32)
    for p in range(width // LANES):
        at = (p + HALO) * rows
        line[at : at + rows, :] = v[:, LANES * p : LANES * (p + 1)]
    for m in range(tm):
        at = (tiles * m + skip) * rows
        stage[m, c] = line[at : at + size, :].astype(jnp.bfloat16)


def spread(packed, loose, wide, rows, first, count):
    loose[...] = packed.astype(jnp.float32)
    for n in range(loose.shape[0]):
        for p in range(count):
            wide[n, first + p, 0:rows, :] = loose[n, rows * p : rows * (p + 1), :]


def kernel(
    sections, batches, tiles, acts, cot, ws_ref, wt_ref, out, spatial, temporal,
    x_stage, g_stage, x_buf, g_buf, r_buf, o_buf, home, fwd, back, time, acc, acc_t, ds,
    w_send, w_recv, w_piece, w_full,
    line, x_loose, g_loose, o_loose, x_wide, g_wide,
    x_sem, g_sem, z_sem, o_sem, w_sem, f_sem,
):
    tm = x_stage.shape[0]
    chains, frame_rows, width = acts.shape
    chans = ws_ref.shape[-1]
    pairs = x_wide.shape[1]
    tile_rows = o_buf.shape[2]
    group = tm * batches
    section, me, core = [lax.axis_index(a) for a in ("section", "tm", "batch")]
    rank = me * batches + core

    def member(e):
        other = lax.rem(rank + e, group)
        return other, (section, other // batches, lax.rem(other, batches))

    def peer(d):
        other = lax.rem(me + d, tm)
        return other, (section, other, core)

    barrier = pltpu.get_barrier_semaphore()
    for e in range(1, group):
        pl.semaphore_signal(barrier, inc=1, device_id=member(e)[1], device_id_type=MESH)

    @pl.when(section > 0)
    def _():
        pl.semaphore_signal(barrier, inc=1, device_id=(section - 1, me, core), device_id_type=MESH)

    @pl.when(section < sections - 1)
    def _():
        pl.semaphore_signal(barrier, inc=1, device_id=(section + 1, me, core), device_id_type=MESH)

    @pl.when(section == sections - 1)
    def _():
        for d in range(1, tm):
            device = (sections - 2, peer(d)[0], core)
            pl.semaphore_signal(barrier, inc=1, device_id=device, device_id_type=MESH)

    @pl.when(section == sections - 2)
    def _():
        for d in range(1, tm):
            device = (sections - 1, peer(d)[0], core)
            pl.semaphore_signal(barrier, inc=1, device_id=device, device_id_type=MESH)

    def copy(src, dst, sems, at, device):
        return pltpu.make_async_remote_copy(
            src_ref=src, dst_ref=dst, send_sem=sems.at[(0,) + at], recv_sem=sems.at[(1,) + at],
            device_id=device, device_id_type=MESH,
        )

    def x_copy(c, d):
        other, device = peer(d)
        return copy(x_stage.at[other, c], x_buf.at[c, me], x_sem, (c, d - 1), device)

    def g_copy(c, d):
        other, _ = peer(d)
        device = (sections - 1, other, core)
        return copy(g_stage.at[other, c], g_buf.at[c, me], g_sem, (c, d - 1), device)

    def z_copy(c):
        return copy(r_buf.at[c], g_buf.at[c], z_sem, (c,), (lax.max(section - 1, 0), me, core))

    def o_copy(c, d):
        other, device = peer(d)
        return copy(o_buf.at[c, other], home.at[c, me], o_sem, (c, d - 1), device)

    def w_copy(e):
        other, device = member(e)
        return copy(w_send.at[other], w_recv.at[rank], w_sem, (e - 1,), device)

    def f_copy(e):
        return copy(w_piece, w_full.at[rank], f_sem, (e - 1,), member(e)[1])

    line[...] = jnp.zeros_like(line)
    x_wide[...] = jnp.zeros_like(x_wide)
    g_wide[...] = jnp.zeros_like(g_wide)
    g_loose[...] = jnp.zeros_like(g_loose)
    pack(acts[0], x_stage, 0, tiles, line, 0)

    @pl.when(section >= sections - 2)
    def _():
        pack(cot[0], g_stage, 0, tiles, line, 1)

    more = (section > 0).astype(jnp.int32) + (section < sections - 1).astype(jnp.int32)
    more += (section >= sections - 2).astype(jnp.int32) * (tm - 1)
    pl.semaphore_wait(barrier, group - 1 + more)

    def send(c, carry):
        @pl.when(c > 0)
        def _():
            pack(acts[c], x_stage, c, tiles, line, 0)

            @pl.when(section >= sections - 2)
            def _():
                pack(cot[c], g_stage, c, tiles, line, 1)

        for d in range(1, tm):
            x_copy(c, d).start()
        x_buf[c, me] = x_stage[me, c]

        @pl.when(section == sections - 1 - lax.rem(c, 2))
        def _():
            for d in range(1, tm):
                g_copy(c, d).start()

        @pl.when(section == sections - 1)
        def _():
            g_buf[c, me] = g_stage[me, c]

        return carry

    lax.fori_loop(0, chains, send, 0)
    set_weights(ws_ref, wt_ref, fwd, back, time)
    acc[...] = jnp.zeros_like(acc)
    acc_t[...] = jnp.zeros_like(acc_t)

    shape = (tm, pairs, ROWS, LANES)
    blank = jnp.zeros((1, pairs, ROWS, LANES), jnp.float32)
    centre = slice(HALO, HALO + tiles)

    def turn(c, carry):
        for d in range(1, tm):
            x_copy(c, d).wait_recv()
        spread(x_buf[c], x_loose, x_wide, frame_rows, 0, pairs)
        x = x_wide[...]
        xx = jnp.concatenate([x, neighbours(x)], axis=3)
        y = mm(flat(xx).astype(jnp.bfloat16), fwd[...], ((1,), (0,)))
        part = [y[:, LANES * i : LANES * (i + 1)].reshape(-1, ROWS, LANES) for i in range(3)]
        z = part[1] + pltpu.roll(part[0], 1, 1) + pltpu.roll(part[2], ROWS - 1, 1)
        z = z.reshape(shape)
        sig = jax.nn.sigmoid(z)
        h = z * sig
        slope = sig * (1.0 + z * (1.0 - sig))

        @pl.when(section == sections - 1)
        def _():
            for d in range(1, tm):
                g_copy(c, d).wait_recv()

        @pl.when(section < sections - 1)
        def _():
            z_copy(c).wait_recv()

        spread(g_buf[c], g_loose, g_wide, frame_rows, 1, pairs - 2)
        g = g_wide[...]
        g3 = jnp.concatenate(
            [
                jnp.concatenate([g[1:], blank], axis=0),
                g,
                jnp.concatenate([blank, g[:-1]], axis=0),
            ],
            axis=3,
        )
        gh = mm(flat(g3).astype(jnp.bfloat16), time[...], ((1,), (1,))).astype(jnp.bfloat16)
        gz = (gh.astype(jnp.float32).reshape(shape) * slope).astype(jnp.bfloat16)
        gz = gz.astype(jnp.float32)
        flat_gz = gz.reshape(-1, ROWS, LANES)
        gg = [
            pltpu.roll(flat_gz, ROWS - 1, 1).reshape(shape),
            gz,
            pltpu.roll(flat_gz, 1, 1).reshape(shape),
        ]
        sides = []
        for v in gg:
            sides += [v, neighbours(v)]
        sides = jnp.concatenate(sides, axis=3).astype(jnp.bfloat16)
        inner = mm(flat(sides), back[...], ((1,), (1,))).reshape(shape)
        place = me * tiles - HALO + lax.broadcasted_iota(jnp.int32, shape, 1)
        row = lax.broadcasted_iota(jnp.int32, shape, 2)
        inside = (place >= 0) & (place < width // LANES) & (row < frame_rows)
        result = jnp.where(inside, g + inner, 0.0)
        for n in range(tm):
            for p in range(pairs - 2):
                at = frame_rows * p
                g_loose[n, at : at + frame_rows, :] = result[n, p + 1, 0:frame_rows]
        r_buf[c] = g_loose[...].astype(jnp.bfloat16)

        @pl.when(section > 0)
        def _():
            z_copy(c).start()

        at = (HALO - 1) * frame_rows
        o_buf[c] = g_loose[:, at : at + tile_rows, :].astype(jnp.bfloat16)
        for d in range(1, tm):
            o_copy(c, d).start()
        home[c, me] = o_buf[c, me]
        hc = flat(h[:, centre]).astype(jnp.bfloat16)
        acc_t[...] += mm(hc, flat(g3[:, centre]).astype(jnp.bfloat16), ((0,), (0,)))
        gc = jnp.concatenate([v[:, centre] for v in gg], axis=3).astype(jnp.bfloat16)
        acc[...] += mm(flat(xx[:, centre]).astype(jnp.bfloat16), flat(gc), ((0,), (0,)))
        return carry

    lax.fori_loop(0, chains, turn, 0)

    taps = taps_of(acc[...], acc_t[...], chans)
    for k in range(6):
        ds[k * chans : (k + 1) * chans, :] = jnp.concatenate([taps[2 * k], taps[2 * k + 1]], axis=1)
    rows = w_send.shape[1]
    for k in range(group):
        w_send[k] = ds[k * rows : (k + 1) * rows, :].astype(jnp.bfloat16)
    for e in range(1, group):
        w_copy(e).start()
    w_recv[rank] = w_send[rank]

    def unpack(c, carry):
        for d in range(1, tm):
            o_copy(c, d).wait_recv()
        o_loose[...] = home[c].astype(jnp.float32)
        cut = [
            o_loose[m, frame_rows * p : frame_rows * (p + 1), :]
            for m in range(tm)
            for p in range(tiles)
        ]
        out[c] = jnp.concatenate(cut, axis=1).astype(jnp.bfloat16)
        return carry

    lax.fori_loop(0, chains - 1, unpack, 0)
    for e in range(1, group):
        w_copy(e).wait_recv()
    w_piece[...] = jnp.sum(w_recv[...].astype(jnp.float32), axis=0)
    for e in range(1, group):
        f_copy(e).start()
    w_full[rank] = w_piece[...]
    unpack(chains - 1, 0)

    for e in range(1, group):
        f_copy(e).wait_recv()
    for k in range(group):
        ds[k * rows : (k + 1) * rows, :] = w_full[k]
    for t in range(12):
        both = ds[(t // 2) * chans : (t // 2 + 1) * chans, :]
        half = both[:, (t % 2) * chans : (t % 2 + 1) * chans]
        if t < 9:
            spatial[t] = half
        else:
            temporal[t - 9] = half

    def finish(c, carry):
        for d in range(1, tm):
            x_copy(c, d).wait_send()
            o_copy(c, d).wait_send()

        @pl.when(section == sections - 1 - lax.rem(c, 2))
        def _():
            for d in range(1, tm):
                g_copy(c, d).wait_send()

        @pl.when(section > 0)
        def _():
            z_copy(c).wait_send()

        return carry

    lax.fori_loop(0, chains, finish, 0)
    for e in range(1, group):
        w_copy(e).wait_send()
        f_copy(e).wait_send()


def body(acts, cot, spatial_weight, temporal_weight):
    sections, tm, batches = [lax.axis_size(a) for a in ("section", "tm", "batch")]
    micro, local, rows, width = cot.shape
    chans = spatial_weight.shape[-1]
    chains = micro * local
    group = tm * batches
    tiles = width // LANES // tm
    pairs = tiles + 2 * HALO
    pairs += pairs % 2
    x_rows, g_rows, tile_rows = [-(-n * rows // 16) * 16 for n in (pairs, pairs - 2, tiles)]
    piece = 6 * chans // group
    bf16, f32 = jnp.bfloat16, jnp.float32
    vmem, dma = pltpu.VMEM, pltpu.SemaphoreType.DMA
    grad, spatial, temporal = pl.pallas_call(
        functools.partial(kernel, sections, batches, tiles),
        out_shape=[
            jax.ShapeDtypeStruct((chains, rows, width), bf16),
            jax.ShapeDtypeStruct((9, chans, chans), f32),
            jax.ShapeDtypeStruct((3, chans, chans), f32),
        ],
        in_specs=[pl.BlockSpec(memory_space=vmem)] * 4,
        out_specs=[pl.BlockSpec(memory_space=vmem)] * 3,
        scratch_shapes=[
            vmem((tm, chains, x_rows, LANES), bf16),
            vmem((tm, chains, g_rows, LANES), bf16),
            vmem((chains, tm, x_rows, LANES), bf16),
            vmem((chains, tm, g_rows, LANES), bf16),
            vmem((chains, tm, g_rows, LANES), bf16),
            vmem((chains, tm, tile_rows, LANES), bf16),
            vmem((chains, tm, tile_rows, LANES), bf16),
            vmem((2 * LANES, 3 * LANES), bf16),
            vmem((LANES, 6 * LANES), bf16),
            vmem((LANES, 3 * LANES), bf16),
            vmem((2 * LANES, 3 * LANES), f32),
            vmem((LANES, 3 * LANES), f32),
            vmem((6 * chans, LANES), f32),
            vmem((group, piece, LANES), bf16),
            vmem((group, piece, LANES), bf16),
            vmem((piece, LANES), f32),
            vmem((group, piece, LANES), f32),
            vmem(((width // LANES + HALO + pairs) * rows + 16, LANES), f32),
            vmem((tm, x_rows, LANES), f32),
            vmem((tm, g_rows, LANES), f32),
            vmem((tm, tile_rows, LANES), f32),
            vmem((tm, pairs, ROWS, LANES), f32),
            vmem((tm, pairs, ROWS, LANES), f32),
            dma((2, chains, tm - 1)),
            dma((2, chains, tm - 1)),
            dma((2, chains)),
            dma((2, chains, tm - 1)),
            dma((2, group - 1)),
            dma((2, group - 1)),
        ],
        compiler_params=pltpu.CompilerParams(
            collective_id=0, has_side_effects=True, vmem_limit_bytes=56 * 2**20
        ),
    )(acts.reshape(chains, rows, width), cot.reshape(chains, rows, width), spatial_weight[0], temporal_weight[0])
    return grad.reshape(acts.shape), spatial[None], temporal[None]


def solution(mesh):
    in_specs = (
        P("section", "batch", "tm", None, None),
        P("batch", "tm", None, None),
        P("section", None, None, None),
        P("section", None, None, None),
    )
    out_specs = (
        P("section", "batch", "tm", None, None),
        P("section", None, None, None),
        P("section", None, None, None),
    )
    return jax.shard_map(body, mesh=mesh, in_specs=in_specs, out_specs=out_specs, check_vma=False)
```
